256 devices in a mesh: grp: 4 (over x_lo, core), dp: 64 (over x_hi, y, z).
Axes of the slice: x: 4 (x_hi: 2, x_lo: 2; x = x_hi * 2 + x_lo), y: 4, z: 8, core: 2. Of those that a mesh axis runs over, the one named last changes fastest.
Arguments:
- activations: bfloat16 [2, 131072, 768], P(None, ('grp', 'dp')), may hold values from -300 to 300
- back_grads: bfloat16 [2, 131072, 768], P(None, ('grp', 'dp')), may hold values from -300 to 300
- grads: float32 [2, 768, 768], P(None, 'dp'), may hold values from -6 to 6
- owners: int32 [4], replicated, may hold values from 0 to 3, as said below
Outputs:
- preconditioned: float32 [2, 768, 768], P(None, 'dp', 'grp')
- owner_store: float32 [8, 768, 768], P('grp', 'dp')
The draws below stay inside these ranges and needn't reach their ends.
Inputs may be any that keep to these rules, and one draw needn't show every extreme that they name: `owners`: one group owns 2 factors, two groups own one factor each, and every other group owns none.
All inputs are finite; a program needn't handle non-finite values. Where the reference program divides by a largest or mean magnitude, that divisor is 1e-20 or more.
Results may differ from the reference program's by a relative error of at most 0.004.
Values may be sent and summed in bfloat16 or wider, within the bound.
No kernel may reach another device: no remote copies, remote signals or barrier semaphores. Data moves between devices by JAX's collectives and lax.ppermute only.
A program may use at most 64 MiB of HBM per device.

```python
import math
import jax
import jax.numpy as jnp
from jax import lax

FEAT = 768
LAYERS = 2
ITERS = 4
CAP = 2
TOK_DEV = 512
NFAC = 4
TOKENS = 131072
N_GRP = 4


def token_rows(key, scale_low, scale_high):
    subkeys = jax.random.split(key, 5)
    full_shape = (LAYERS, TOKENS, FEAT)
    gauss_part = jnp.clip(jax.random.normal(subkeys[0], full_shape, jnp.float32), -4.0, 4.0)
    noise_base = gauss_part
    mixed = noise_base + 0.6 * jnp.roll(noise_base, -1, axis=2) + 0.45 * jnp.roll(noise_base, FEAT // 2, axis=2)
    scales = jnp.exp(jax.random.uniform(subkeys[3], (LAYERS, 1, FEAT), jnp.float32, math.log(scale_low), math.log(scale_high)))
    device_count = TOKENS // TOK_DEV
    span_width = max(1, FEAT // device_count)
    block_count = FEAT // span_width
    rotation = jax.random.randint(subkeys[4], (), 0, FEAT)
    device_of = jnp.arange(TOKENS) // TOK_DEV
    feature_pos = (jnp.arange(FEAT) - rotation) % FEAT
    lifted = feature_pos[None, :] // span_width == device_of[:, None] % block_count
    boost_factor = jnp.where(lifted, 8.0, 1.0)
    return (mixed * scales * boost_factor[None]).astype(jnp.bfloat16)


def draw_activations(key, part):
    key = jax.random.fold_in(key, 5)
    return token_rows(key, 0.5, 4.0)


def draw_back_grads(key, part):
    key = jax.random.fold_in(key, 9)
    return token_rows(key, 0.5, 4.0)


def draw_owners(key, part):
    key = jax.random.fold_in(key, 17)
    key_order, key_groups = jax.random.split(key)
    factor_order = jax.random.permutation(key_order, NFAC)
    groups = jax.random.permutation(key_groups, N_GRP)
    targets = groups[jnp.maximum(jnp.arange(NFAC) - 1, 0)]
    return jnp.zeros((NFAC,), jnp.int32).at[factor_order].set(targets.astype(jnp.int32))


def shard_levels(rng, extent, pieces, least, top_value):
    loudness, own = 1.0, jax.random.fold_in(rng, 6)
    for position, shards_of in pieces:
        steps = jnp.exp(jax.random.uniform(jax.random.fold_in(own, position), (shards_of,), jnp.float32, least / len(pieces), top_value / len(pieces)))
        loudness = loudness * jnp.repeat(steps, extent[position] // shards_of).reshape([-1 if axis == position else 1 for axis in range(len(extent))])
    return loudness


def centred(own_key, extent, width, reach, shards=(), held_as=jnp.bfloat16):
    loudness = shard_levels(own_key, extent, shards, -0.22, 0.18) if shards else 1.0
    array = jax.random.normal(own_key, extent, jnp.float32) * width * loudness
    return jnp.minimum(jnp.maximum(array, -reach), reach).astype(held_as)


def setup_inputs(seed: int = 0) -> dict:
    splits = jax.random.split(jax.random.key(seed), 5)
    return {
        "activations": draw_activations(jax.random.fold_in(splits[4], 71), 0),
        "back_grads": draw_back_grads(jax.random.fold_in(splits[4], 71), 0),
        "grads": centred(splits[2], (LAYERS, FEAT, FEAT), 1.0, 6.0, ((1, 64),), jnp.float32),
        "owners": draw_owners(jax.random.fold_in(splits[4], 71), 0),
    }


DAMPING = 0.1


def newton_inverse(factor):
    identity = jnp.eye(factor.shape[0], dtype=jnp.float32)
    damped = factor + DAMPING * identity
    bound_max = jnp.max(jnp.sum(jnp.abs(damped), axis=1))
    low_damped = damped.astype(jnp.bfloat16)
    iterate = identity * (1.0 / bound_max)
    for sweep in range(ITERS):
        iterate_low = iterate.astype(jnp.bfloat16)
        image_low = jnp.dot(low_damped, iterate_low, preferred_element_type=jnp.float32).astype(jnp.bfloat16)
        iterate = 2.0 * iterate - jnp.dot(iterate_low, image_low, preferred_element_type=jnp.float32)
    return iterate


def reference(activations, back_grads, grads, owners):
    inverses = []
    for layer_idx in range(LAYERS):
        for source in (activations, back_grads):
            samples = source[layer_idx]
            factor = jnp.dot(samples.T, samples, preferred_element_type=jnp.float32) / TOKENS
            inverses.append(newton_inverse(factor))
    stacked = jnp.stack(inverses)
    factor_ids = jnp.arange(NFAC).astype(jnp.int32)
    same_owner = owners[:, None] == owners[None, :]
    earlier = factor_ids[None, :] < factor_ids[:, None]
    owner_rank = jnp.sum((same_owner & earlier).astype(jnp.int32), axis=1).astype(jnp.int32)
    slot_ids = (owners * CAP + owner_rank).astype(jnp.int32)
    owner_store = jnp.zeros((N_GRP * CAP, FEAT, FEAT), jnp.float32).at[slot_ids].set(stacked)
    results = []
    for layer_idx in range(LAYERS):
        mapped = jnp.dot(grads[layer_idx], stacked[2 * layer_idx], precision=lax.Precision.HIGHEST)
        results.append(jnp.dot(stacked[2 * layer_idx + 1].T, mapped, precision=lax.Precision.HIGHEST))
    return jnp.stack(results), owner_store
```

```python
import functools
import jax
import jax.numpy as jnp
from jax import lax
from jax.experimental import pallas as pl
from jax.experimental.pallas import tpu as pltpu
from jax.sharding import Mesh
from jax.sharding import PartitionSpec as P

CAP = 2
DAMPING = 0.1
TILE = 128
WIDE = 2 * TILE
X = ("xl", "xh")
XYL = ("xl", "xh", "y", "zl")
Z = ("zh", "zl")
bf16 = jnp.bfloat16
f32 = jnp.float32


def upper(nb):
    return [(i, j) for i in range(nb) for j in range(i, nb)]


def dot(a, b, ca=1, cb=0):
    return lax.dot_general(a, b, (((ca,), (cb,)), ((), ())), preferred_element_type=f32)


def other_layer_kernel(core_ref, act, bg, out, sems):
    copies = []
    for f, src in enumerate((act, bg)):
        copies.append(pltpu.make_async_copy(src.at[1 - core_ref[0]], out.at[f], sems.at[f]))
        copies[f].start()
    for c in copies:
        c.wait()


def factor_kernel(core_ref, act, bg, peer, out, tokens, made, sems):
    tok, feat = act.shape[1:]
    copies = []
    for f, own in enumerate((act, bg)):
        a = pltpu.make_async_copy(own.at[core_ref[0]], tokens.at[f, pl.ds(0, tok)], sems.at[f, 0])
        b = pltpu.make_async_copy(peer.at[f], tokens.at[f, pl.ds(tok, tok)], sems.at[f, 1])
        a.start()
        b.start()
        copies.append((a, b))
    k = 0
    done = []
    for f in range(2):
        for c in copies[f]:
            c.wait()
        for lo in range(0, feat, WIDE):
            r = dot(tokens[f, :, lo : lo + WIDE], tokens[f, :, lo:], 0, 0)
            for top in (0, TILE):
                for left in range(top, feat - lo, TILE):
                    made[k * TILE : (k + 1) * TILE, :] = r[top : top + TILE, left : left + TILE].astype(bf16)
                    k += 1
        part = pl.ds(f * (made.shape[0] // 2), made.shape[0] // 2)
        done.append(pltpu.make_async_copy(made.at[part], out.at[part], sems.at[f, 2]))
        done[f].start()
    for c in done:
        c.wait()


def halves(u):
    hi = u.astype(bf16)
    return jnp.concatenate([hi, (u - hi.astype(f32)).astype(bf16)], axis=0)


def times(two, m):
    r = dot(two, m)
    n = two.shape[0] // 2
    return r[:n] + r[n:]


def chain(u, mats, inv):
    u = 2.0 * u - times(halves(u), mats[0]) * inv
    u = 2.0 * u - times(halves(u), mats[1])
    u = 2.0 * u - times(halves(u), mats[2])
    t = u - times(halves(u), mats[2])
    t = t - times(halves(t), mats[2])
    return (u + t) * inv


def eye_rows(at, count, own, feat):
    r = lax.broadcasted_iota(jnp.int32, (own, feat), 0)
    c = lax.broadcasted_iota(jnp.int32, (own, feat), 1)
    return jnp.where((c == at * count + r) & (r < count), 1.0, 0.0).astype(f32)


def finish_kernel(place, blocks, grads, order, rows_out, pre_out, mats):
    feat = order.shape[0]
    pairs = upper(feat // TILE)

    def put(dst, i, j, block):
        n = block.shape[0]
        dst[i * n : (i + 1) * n, j * n : (j + 1) * n] = block
        if i != j:
            dst[j * n : (j + 1) * n, i * n : (i + 1) * n] = block.T

    def square(src, dst, one, two):
        for i in range(feat // WIDE):
            lo = i * WIDE
            r = dot(src[lo : lo + WIDE, :], src[:, lo:])
            for j in range(i, feat // WIDE):
                old = src[lo : lo + WIDE, j * WIDE : (j + 1) * WIDE].astype(f32)
                new = one * old - two * r[:, (j - i) * WIDE : (j - i + 1) * WIDE]
                put(dst, i, j, new.astype(bf16))

    def matrices(f, mats):
        for n, (i, j) in enumerate(pairs):
            k = f * len(pairs) + n
            put(mats.at[0], i, j, blocks[k * TILE : (k + 1) * TILE, :])
        sums = jnp.sum(jnp.abs(mats[0].astype(f32)), axis=1, keepdims=True)
        inv = 1.0 / jnp.max(sums, axis=0, keepdims=True)
        square(mats.at[0], mats.at[1], 2.0 * inv, inv * inv)
        square(mats.at[1], mats.at[2], 2.0, 1.0)
        return inv

    even, odd = mats.at[0], mats.at[1]
    odd_inv = matrices(1, odd)
    even_inv = matrices(0, even)
    own = rows_out.shape[1]
    eye = eye_rows(place[0], place[2], own, feat)
    rows = chain(jnp.concatenate([eye, eye_rows(place[1], place[2], own, feat)], axis=0), odd, odd_inv)
    rows_out[1] = rows[:own]
    left = dot(halves(rows), order[...]).astype(bf16)
    v = times(left, grads[...])
    both = chain(jnp.concatenate([v, eye], axis=0), even, even_inv)
    pre_out[...] = both[: 2 * own]
    rows_out[0] = both[2 * own :]


def shards(activations, back_grads, grads, owners):
    nxl, ncore, nxh, ny, nzh, nzl = (lax.axis_size(a) for a in ("xl", "core", "xh", "y", "zh", "zl"))
    xl, core, xh, y, zh, zl = (lax.axis_index(a) for a in ("xl", "core", "xh", "y", "zh", "zl"))
    nz = nzh * nzl
    layers, tok, feat = activations.shape
    nb = feat // TILE
    nblk = len(upper(nb))
    nrow = grads.shape[1]
    groups = nxl * ncore
    cols = feat // groups
    total = tok * nxl * ncore * nxh * ny * nz
    group = xl * ncore + core
    dp = (xh * ny + y) * nz + zh * nzl + zl
    params = pltpu.CompilerParams(vmem_limit_bytes=48 << 20)
    sm = pl.BlockSpec(memory_space=pltpu.SMEM)
    vm = pl.BlockSpec(memory_space=pltpu.VMEM)
    anywhere = pl.BlockSpec(memory_space=pl.ANY)

    swap = [(0, 1), (1, 0)]
    send = pl.pallas_call(
        other_layer_kernel,
        out_shape=jax.ShapeDtypeStruct((2, tok, feat), bf16),
        in_specs=[sm, anywhere, anywhere],
        out_specs=vm,
        scratch_shapes=[pltpu.SemaphoreType.DMA((2,))],
        compiler_params=pltpu.CompilerParams(vmem_limit_bytes=60 << 20),
        cost_estimate=pl.CostEstimate(flops=0, bytes_accessed=8 * tok * feat, transcendentals=0),
    )(core.reshape(1), activations, back_grads)
    peer = lax.ppermute(send, "core", swap)
    def along(a, axis):
        size = lax.axis_size(axis)
        return [a] + [lax.ppermute(a, axis, [(i, i ^ e) for i in range(size)]) for e in range(1, size)]

    g = lax.dynamic_index_in_dim(grads, core, 0, keepdims=False).astype(bf16)
    g = along(g, "zh")

    partial = pl.pallas_call(
        factor_kernel,
        out_shape=jax.ShapeDtypeStruct((2 * nblk * TILE, TILE), bf16),
        in_specs=[sm] + [anywhere] * 3,
        out_specs=anywhere,
        scratch_shapes=[
            pltpu.VMEM((2, 2 * tok, feat), bf16),
            pltpu.VMEM((2 * nblk * TILE, TILE), bf16),
            pltpu.SemaphoreType.DMA((2, 3)),
        ],
        compiler_params=pltpu.CompilerParams(vmem_limit_bytes=60 << 20),
        cost_estimate=pl.CostEstimate(flops=4 * tok * 2 * feat * feat, bytes_accessed=8 * tok * feat, transcendentals=0),
    )(core.reshape(1), activations, back_grads, peer)

    share = nxl * nxh * ny * nzl
    rows = 2 * nblk * TILE // share
    partial, g = lax.optimization_barrier((partial, g))
    terms = lax.all_to_all(partial.reshape(share, rows, TILE), XYL, 0, 0, tiled=True)
    g = jnp.stack(g)
    g = [g, lax.ppermute(g, X, [(0, 3), (3, 0), (1, 2), (2, 1)])]
    terms, g = lax.optimization_barrier((terms, g))

    mine = jnp.sum(terms.astype(f32), axis=0).astype(bf16)
    mine = jnp.broadcast_to(mine[None], (nzh, rows, TILE))
    mine, g = lax.optimization_barrier((mine, g))
    stack = lax.all_to_all(mine, "zh", 0, 0, tiled=True)
    g = along(jnp.stack(g), "y")
    stack, g = lax.optimization_barrier((stack, g))
    factor = jnp.sum(stack.astype(f32), axis=0) / float(total)
    at = (((xl * nxh + xh) * ny + y) * nzl + zl) * rows + jnp.arange(rows)
    diagonal = functools.reduce(
        jnp.logical_or, [(at // TILE) % nblk == n for n, (i, j) in enumerate(upper(nb)) if i == j]
    )
    on = diagonal[:, None] & ((at % TILE)[:, None] == jnp.arange(TILE)[None, :])
    damped = (factor + jnp.where(on, DAMPING, 0.0)).astype(bf16)
    blocks = lax.all_to_all(jnp.broadcast_to(damped[None], (share, rows, TILE)), XYL, 0, 0, tiled=True)
    half = feat // nzl
    part = jnp.stack(g).reshape(half, feat)
    k = jnp.arange(half)
    step = k // nrow
    from_zh = (step % nzh) ^ zh
    from_xh = (step // nzh % nxh) ^ xh
    from_y = (step // (nzh * nxh)) ^ y
    to = (((from_xh * ny + from_y) * nzh + from_zh) * nzl + zl) * nrow + k % nrow
    order = (jnp.arange(feat)[:, None] == to[None, :]).astype(bf16)

    own = 16
    inv_rows, pre = pl.pallas_call(
        finish_kernel,
        out_shape=(jax.ShapeDtypeStruct((2, own, feat), f32), jax.ShapeDtypeStruct((2 * own, feat), f32)),
        in_specs=[sm, vm, vm, vm],
        out_specs=(vm, vm),
        scratch_shapes=[pltpu.VMEM((2, 3, feat, feat), bf16)],
        compiler_params=params,
        cost_estimate=pl.CostEstimate(flops=6 * feat**3, bytes_accessed=8 * feat * feat, transcendentals=0),
    )(jnp.stack([dp, dp ^ 1, jnp.int32(nrow)]), blocks.reshape(2 * nblk * TILE, TILE), part, order)
    inv_rows = inv_rows[:, :nrow]

    def columns(rows, of):
        return lax.dynamic_slice_in_dim(rows, (xl * ncore + of) * cols, cols, 1)

    mine, theirs = pre[:nrow], pre[own : own + nrow]
    packed = jnp.concatenate([inv_rows[0], inv_rows[1], columns(mine, 1 - core)], axis=1)
    got = lax.ppermute(packed, "core", swap)
    near = lax.ppermute(columns(theirs, core), "zl", swap)
    cross = lax.ppermute(columns(theirs, 1 - core), ("core", "zl"), [(0, 3), (3, 0), (1, 2), (2, 1)])
    got_rows = jnp.stack([got[:, :feat], got[:, feat : 2 * feat]])
    got_pre = got[:, 2 * feat :] + cross
    mine_pre = columns(mine, core) + near
    first = core == 0
    out = jnp.stack([jnp.where(first, mine_pre, got_pre), jnp.where(first, got_pre, mine_pre)])
    rows_all = jnp.concatenate([jnp.where(first, inv_rows, got_rows), jnp.where(first, got_rows, inv_rows)])
    ids = jnp.arange(2 * layers)
    rank = jnp.sum(((owners[:, None] == owners[None, :]) & (ids[None, :] < ids[:, None])).astype(jnp.int32), axis=1)
    slots = []
    for slot in range(CAP):
        acc = jnp.zeros((nrow, feat), f32)
        for f in range(2 * layers):
            acc = jnp.where((owners[f] == group) & (rank[f] == slot), rows_all[f], acc)
        slots.append(acc)
    return out, jnp.stack(slots)


def solution(mesh):
    split = Mesh(mesh.devices.reshape(2, 2, 2, 4, 4, 2), ("xl", "core", "xh", "y", "zh", "zl"))
    grp, dp = ("xl", "core"), ("xh", "y", "zh", "zl")
    return jax.shard_map(
        shards,
        mesh=split,
        in_specs=(P(None, grp + dp, None), P(None, grp + dp, None), P(None, dp, None), P()),
        out_specs=(P(None, dp, grp), P(grp, dp, None)),
        check_vma=False,
    )
```

```python
import functools
import jax
import jax.numpy as jnp
from jax import lax
from jax.experimental import pallas as pl
from jax.experimental.pallas import tpu as pltpu
from jax.sharding import Mesh
from jax.sharding import PartitionSpec as P

CAP = 2
DAMPING = 0.1
TILE = 128
WIDE = 2 * TILE
X = ("xl", "xh")
XYL = ("xl", "xh", "y", "zl")
Z = ("zh", "zl")
bf16 = jnp.bfloat16
f32 = jnp.float32


def upper(nb):
    return [(i, j) for i in range(nb) for j in range(i, nb)][:-1]


def dot(a, b, ca=1, cb=0):
    return lax.dot_general(a, b, (((ca,), (cb,)), ((), ())), preferred_element_type=f32)


def factor_kernel(core_ref, act, bg, peer_act, peer_bg, out, tokens, made, sems):
    tok, feat = act.shape[1:]
    copies = []
    for f, (own, peer) in enumerate(((act, peer_act), (bg, peer_bg))):
        a = pltpu.make_async_copy(own.at[core_ref[0]], tokens.at[f, pl.ds(0, tok)], sems.at[f, 0])
        b = pltpu.make_async_copy(peer.at[core_ref[0]], tokens.at[f, pl.ds(tok, tok)], sems.at[f, 1])
        a.start()
        b.start()
        copies.append((a, b))
    pairs = upper(feat // TILE)
    mid = TILE // 2
    done = []
    for f in range(2):
        for c in copies[f]:
            c.wait()
        for lo in range(0, feat, WIDE):
            r = dot(tokens[f, :, lo : lo + WIDE], tokens[f, :, lo:], 0, 0)
            for top in (0, TILE):
                for left in range(top, feat - lo, TILE):
                    at = (lo + top) // TILE, (lo + left) // TILE
                    block = r[top : top + TILE, left : left + TILE].astype(bf16)
                    if at in pairs:
                        k = f * len(pairs) + pairs.index(at)
                        made[k * TILE : (k + 1) * TILE, :] = block
        for n, quarter in enumerate((block[:mid, :mid], block[mid:, mid:], block[:mid, mid:])):
            k = f * len(pairs) + pairs.index((n, n))
            made[k * TILE + mid : (k + 1) * TILE, :mid] = quarter
        part = pl.ds(f * (made.shape[0] // 2), made.shape[0] // 2)
        done.append(pltpu.make_async_copy(made.at[part], out.at[part], sems.at[f, 2]))
        done[f].start()
    for c in done:
        c.wait()


def halves(u):
    hi = u.astype(bf16)
    return jnp.concatenate([hi, (u - hi.astype(f32)).astype(bf16)], axis=0)


def times(two, m):
    r = dot(two, m)
    n = two.shape[0] // 2
    return r[:n] + r[n:]


def chain(u, mats, inv):
    u = 2.0 * u - times(halves(u), mats[0]) * inv
    u = 2.0 * u - times(halves(u), mats[1])
    u = 2.0 * u - times(halves(u), mats[2])
    t = u - times(halves(u), mats[2])
    t = t - times(halves(t), mats[2])
    return (u + t) * inv


def eye_rows(at, count, own, feat):
    r = lax.broadcasted_iota(jnp.int32, (own, feat), 0)
    c = lax.broadcasted_iota(jnp.int32, (own, feat), 1)
    return jnp.where((c == at * count + r) & (r < count), 1.0, 0.0).astype(f32)


def finish_kernel(place, blocks, grads, order, packed, mine_out, near_out, cross_out, mats):
    feat = order.shape[0]
    pairs = upper(feat // TILE)
    mid = TILE // 2

    def put(dst, i, j, block):
        n = block.shape[0]
        dst[i * n : (i + 1) * n, j * n : (j + 1) * n] = block
        if i != j:
            dst[j * n : (j + 1) * n, i * n : (i + 1) * n] = block.T

    def square(src, dst, one, two):
        for i in range(feat // WIDE):
            lo = i * WIDE
            r = dot(src[lo : lo + WIDE, :], src[:, lo:])
            for j in range(i, feat // WIDE):
                old = src[lo : lo + WIDE, j * WIDE : (j + 1) * WIDE].astype(f32)
                new = one * old - two * r[:, (j - i) * WIDE : (j - i + 1) * WIDE]
                put(dst, i, j, new.astype(bf16))

    def matrices(f, mats):
        corner = []
        for n, (i, j) in enumerate(pairs):
            k = f * len(pairs) + n
            block = blocks[k * TILE : (k + 1) * TILE, :]
            if i == j and i < 3:
                up = block[:mid, mid:]
                corner.append(block[mid:, :mid])
                low = jnp.concatenate([up.T, block[mid:, mid:]], axis=1)
                block = jnp.concatenate([block[:mid], low], axis=0)
            put(mats.at[0], i, j, block)
        first, last, up = corner
        low = jnp.concatenate([up.T, last], axis=1)
        block = jnp.concatenate([jnp.concatenate([first, up], axis=1), low], axis=0)
        put(mats.at[0], feat // TILE - 1, feat // TILE - 1, block)
        sums = jnp.sum(jnp.abs(mats[0].astype(f32)), axis=1, keepdims=True)
        inv = 1.0 / jnp.max(sums, axis=0, keepdims=True)
        square(mats.at[0], mats.at[1], 2.0 * inv, inv * inv)
        square(mats.at[1], mats.at[2], 2.0, 1.0)
        return inv

    even, odd = mats.at[0], mats.at[1]
    odd_inv = matrices(1, odd)
    own = packed.shape[0]
    cols = mine_out.shape[1]
    eye = eye_rows(place[0], place[2], own, feat)
    rows = chain(jnp.concatenate([eye, eye_rows(place[1], place[2], own, feat)], axis=0), odd, odd_inv)
    packed[:, feat : 2 * feat] = rows[:own]
    even_inv = matrices(0, even)
    left = dot(halves(rows), order[...]).astype(bf16)
    v = times(left, grads[...])
    both = chain(jnp.concatenate([v, eye], axis=0), even, even_inv)
    packed[:, :feat] = both[2 * own :]

    def columns(group):
        out = both[: 2 * own, :cols]
        for n in range(1, feat // cols):
            out = jnp.where(group == n, both[: 2 * own, n * cols : (n + 1) * cols], out)
        return out

    here, there = columns(place[3]), columns(place[4])
    mine_out[...] = here[:own]
    near_out[...] = here[own:]
    cross_out[...] = there[own:]
    packed[:, 2 * feat :] = there[:own]


def output_kernel(owners, place, packed, got, mine, near, cross, result, store):
    nrow, slots, feat = store.shape
    first = place[5] == 0
    own = mine[:nrow] + near[:nrow]
    other = got[:nrow, 2 * feat :] + cross[:nrow]
    result[:, 0, :] = jnp.where(first, own, other)
    result[:, 1, :] = jnp.where(first, other, own)
    rows = []
    for l in range(2):
        for i in range(2):
            a, b = (packed, got) if l == 0 else (got, packed)
            part = slice(i * feat, (i + 1) * feat)
            rows.append(jnp.where(first, a[:nrow, part], b[:nrow, part]))
    for slot in range(slots):
        acc = jnp.zeros((nrow, feat), f32)
        for f, block in enumerate(rows):
            rank = sum(((owners[e] == owners[f]).astype(jnp.int32) for e in range(f)), jnp.int32(0))
            acc = jnp.where((owners[f] == place[3]) & (rank == slot), block, acc)
        store[:, slot, :] = acc


def shards(activations, back_grads, grads, owners):
    nxl, ncore, nxh, ny, nzh, nzl = (lax.axis_size(a) for a in ("xl", "core", "xh", "y", "zh", "zl"))
    xl, core, xh, y, zh, zl = (lax.axis_index(a) for a in ("xl", "core", "xh", "y", "zh", "zl"))
    nz = nzh * nzl
    layers, tok, feat = activations.shape
    nb = feat // TILE
    nblk = len(upper(nb))
    nrow = grads.shape[1]
    groups = nxl * ncore
    cols = feat // groups
    total = tok * nxl * ncore * nxh * ny * nz
    group = xl * ncore + core
    dp = (xh * ny + y) * nz + zh * nzl + zl
    params = pltpu.CompilerParams(vmem_limit_bytes=48 << 20)
    sm = pl.BlockSpec(memory_space=pltpu.SMEM)
    vm = pl.BlockSpec(memory_space=pltpu.VMEM)
    anywhere = pl.BlockSpec(memory_space=pl.ANY)

    swap = [(0, 1), (1, 0)]
    peer = [lax.ppermute(a, "core", swap) for a in (activations, back_grads)]
    def along(a, axis):
        size = lax.axis_size(axis)
        return [a] + [lax.ppermute(a, axis, [(i, i ^ e) for i in range(size)]) for e in range(1, size)]

    g = lax.dynamic_index_in_dim(grads, core, 0, keepdims=False).astype(bf16)
    g = along(g, "zh")

    partial = pl.pallas_call(
        factor_kernel,
        out_shape=jax.ShapeDtypeStruct((2 * nblk * TILE, TILE), bf16),
        in_specs=[sm] + [anywhere] * 4,
        out_specs=anywhere,
        scratch_shapes=[
            pltpu.VMEM((2, 2 * tok, feat), bf16),
            pltpu.VMEM((2 * nblk * TILE, TILE), bf16),
            pltpu.SemaphoreType.DMA((2, 3)),
        ],
        compiler_params=pltpu.CompilerParams(vmem_limit_bytes=60 << 20),
        cost_estimate=pl.CostEstimate(flops=4 * tok * 2 * feat * feat, bytes_accessed=8 * tok * feat, transcendentals=0),
    )(core.reshape(1), activations, back_grads, *peer)

    share = nxl * nxh * ny * nzl
    rows = 2 * nblk * TILE // share
    partial, g = lax.optimization_barrier((partial, g))
    terms = lax.all_to_all(partial.reshape(share, rows, TILE), XYL, 0, 0, tiled=True)
    g = along(jnp.stack(g), "y")
    terms, g = lax.optimization_barrier((terms, g))

    mine = jnp.sum(terms.astype(f32), axis=0).astype(bf16)
    mine, g = lax.optimization_barrier((mine, g))
    stack = along(mine, "zh")
    g = jnp.stack(g)
    g = [g, lax.ppermute(g, X, [(0, 3), (3, 0), (1, 2), (2, 1)])]
    stack, g = lax.optimization_barrier((stack, g))
    pair = [a.astype(f32) + b.astype(f32) for a, b in zip(stack[0::2], stack[1::2])]
    factor = (pair[0] + pair[1]) / float(total)
    at = (((xl * nxh + xh) * ny + y) * nzl + zl) * rows + jnp.arange(rows)
    pairs = upper(nb)

    def within(blocks):
        return functools.reduce(jnp.logical_or, [(at // TILE) % nblk == pairs.index((n, n)) for n in blocks])

    spot = jnp.arange(TILE)[None, :]
    on = within(range(nb - 1))[:, None] & ((at % TILE)[:, None] == spot)
    on |= within((0, 1))[:, None] & ((at % TILE - TILE // 2)[:, None] == spot)
    damped = (factor + jnp.where(on, DAMPING, 0.0)).astype(bf16)
    blocks = lax.all_to_all(jnp.broadcast_to(damped[None], (share, rows, TILE)), XYL, 0, 0, tiled=True)
    half = feat // nzl
    part = jnp.stack(g).reshape(half, feat)
    k = jnp.arange(half)
    step = k // nrow
    from_zh = (step % nzh) ^ zh
    from_y = (step // nzh % ny) ^ y
    from_xh = (step // (nzh * ny)) ^ xh
    to = (((from_xh * ny + from_y) * nzh + from_zh) * nzl + zl) * nrow + k % nrow
    order = (jnp.arange(feat)[:, None] == to[None, :]).astype(bf16)

    own = 16
    place = jnp.stack([dp, dp ^ 1, jnp.int32(nrow), group, xl * ncore + 1 - core, core])
    packed, mine, near, cross = pl.pallas_call(
        finish_kernel,
        out_shape=[jax.ShapeDtypeStruct((own, n), f32) for n in (2 * feat + cols, cols, cols, cols)],
        in_specs=[sm, vm, vm, vm],
        out_specs=[vm] * 4,
        scratch_shapes=[pltpu.VMEM((2, 3, feat, feat), bf16)],
        compiler_params=params,
        cost_estimate=pl.CostEstimate(flops=6 * feat**3, bytes_accessed=8 * feat * feat, transcendentals=0),
    )(place, blocks.reshape(2 * nblk * TILE, TILE), part, order)

    got = lax.ppermute(packed, "core", swap)
    near = lax.ppermute(near, "zl", swap)
    cross = lax.ppermute(cross, ("core", "zl"), [(0, 3), (3, 0), (1, 2), (2, 1)])
    result, store = pl.pallas_call(
        output_kernel,
        out_shape=[jax.ShapeDtypeStruct((nrow, layers, cols), f32), jax.ShapeDtypeStruct((nrow, CAP, feat), f32)],
        in_specs=[sm, sm] + [vm] * 5,
        out_specs=[vm, vm],
        compiler_params=params,
    )(owners, place, packed, got, mine, near, cross)
    return jnp.transpose(result, (1, 0, 2)), jnp.transpose(store, (1, 0, 2))


def solution(mesh):
    split = Mesh(mesh.devices.reshape(2, 2, 2, 4, 4, 2), ("xl", "core", "xh", "y", "zh", "zl"))
    grp, dp = ("xl", "core"), ("xh", "y", "zh", "zl")
    return jax.shard_map(
        shards,
        mesh=split,
        in_specs=(P(None, grp + dp, None), P(None, grp + dp, None), P(None, dp, None), P()),
        out_specs=(P(None, dp, grp), P(grp, dp, None)),
        check_vma=False,
    )
```

```python
import functools
import jax
import jax.numpy as jnp
from jax import lax
from jax.experimental import pallas as pl
from jax.experimental.pallas import tpu as pltpu
from jax.sharding import Mesh
from jax.sharding import PartitionSpec as P

CAP = 2
DAMPING = 0.1
TILE = 128
WIDE = 2 * TILE
X = ("xl", "xh")
XYL = ("xl", "xh", "y", "zl")
Z = ("zh", "zl")
bf16 = jnp.bfloat16
f32 = jnp.float32


def upper(nb):
    return [(i, j) for i in range(nb) for j in range(i, nb)][:-1]


def dot(a, b, ca=1, cb=0):
    return lax.dot_general(a, b, (((ca,), (cb,)), ((), ())), preferred_element_type=f32)


def factor_kernel(core_ref, act, bg, peer_act, peer_bg, out, tokens, made, sems):
    tok, feat = act.shape[1:]
    copies = []
    for f, (own, peer) in enumerate(((act, peer_act), (bg, peer_bg))):
        a = pltpu.make_async_copy(own.at[core_ref[0]], tokens.at[f, pl.ds(0, tok)], sems.at[f, 0])
        b = pltpu.make_async_copy(peer.at[core_ref[0]], tokens.at[f, pl.ds(tok, tok)], sems.at[f, 1])
        a.start()
        b.start()
        copies.append((a, b))
    pairs = upper(feat // TILE)
    mid = TILE // 2
    done = []
    for f in range(2):
        for c in copies[f]:
            c.wait()
        for lo in range(0, feat, WIDE):
            r = dot(tokens[f, :, lo : lo + WIDE], tokens[f, :, lo:], 0, 0)
            for top in (0, TILE):
                for left in range(top, feat - lo, TILE):
                    at = (lo + top) // TILE, (lo + left) // TILE
                    block = r[top : top + TILE, left : left + TILE].astype(bf16)
                    if at in pairs:
                        k = f * len(pairs) + pairs.index(at)
                        made[k * TILE : (k + 1) * TILE, :] = block
        for n, quarter in enumerate((block[:mid, :mid], block[mid:, mid:], block[:mid, mid:])):
            k = f * len(pairs) + pairs.index((n, n))
            made[k * TILE + mid : (k + 1) * TILE, :mid] = quarter
        part = pl.ds(f * (made.shape[0] // 2), made.shape[0] // 2)
        done.append(pltpu.make_async_copy(made.at[part], out.at[part], sems.at[f, 2]))
        done[f].start()
    for c in done:
        c.wait()


def halves(u):
    hi = u.astype(bf16)
    return jnp.concatenate([hi, (u - hi.astype(f32)).astype(bf16)], axis=0)


def times(two, m):
    r = dot(two, m)
    n = two.shape[0] // 2
    return r[:n] + r[n:]


def chain(u, mats, inv):
    u = 2.0 * u - times(halves(u), mats[0]) * inv
    u = 2.0 * u - times(halves(u), mats[1])
    u = 2.0 * u - times(halves(u), mats[2])
    t = u - times(halves(u), mats[2])
    t = t - times(halves(t), mats[2])
    return (u + t) * inv


def eye_rows(at, count, own, feat):
    r = lax.broadcasted_iota(jnp.int32, (own, feat), 0)
    c = lax.broadcasted_iota(jnp.int32, (own, feat), 1)
    return jnp.where((c == at * count + r) & (r < count), 1.0, 0.0).astype(f32)


def finish_kernel(place, blocks, grads, order, packed, mine_out, near_out, cross_out, mats):
    feat = order.shape[0]
    pairs = upper(feat // TILE)
    mid = TILE // 2

    def put(dst, i, j, block):
        n = block.shape[0]
        dst[i * n : (i + 1) * n, j * n : (j + 1) * n] = block
        if i != j:
            dst[j * n : (j + 1) * n, i * n : (i + 1) * n] = block.T

    def square(src, dst, one, two):
        for i in range(feat // WIDE):
            lo = i * WIDE
            r = dot(src[lo : lo + WIDE, :], src[:, lo:])
            for j in range(i, feat // WIDE):
                old = src[lo : lo + WIDE, j * WIDE : (j + 1) * WIDE].astype(f32)
                new = one * old - two * r[:, (j - i) * WIDE : (j - i + 1) * WIDE]
                put(dst, i, j, new.astype(bf16))

    def matrices(f, mats):
        corner = []
        for n, (i, j) in enumerate(pairs):
            k = f * len(pairs) + n
            block = blocks[k * TILE : (k + 1) * TILE, :]
            if i == j and i < 3:
                up = block[:mid, mid:]
                corner.append(block[mid:, :mid])
                low = jnp.concatenate([up.T, block[mid:, mid:]], axis=1)
                block = jnp.concatenate([block[:mid], low], axis=0)
            put(mats.at[0], i, j, block)
        first, last, up = corner
        low = jnp.concatenate([up.T, last], axis=1)
        block = jnp.concatenate([jnp.concatenate([first, up], axis=1), low], axis=0)
        put(mats.at[0], feat // TILE - 1, feat // TILE - 1, block)
        sums = jnp.sum(jnp.abs(mats[0].astype(f32)), axis=1, keepdims=True)
        inv = 1.0 / jnp.max(sums, axis=0, keepdims=True)
        square(mats.at[0], mats.at[1], 2.0 * inv, inv * inv)
        square(mats.at[1], mats.at[2], 2.0, 1.0)
        return inv

    even, odd = mats.at[0], mats.at[1]
    odd_inv = matrices(1, odd)
    own = packed.shape[0]
    cols = mine_out.shape[1]
    eye = eye_rows(place[0], place[2], own, feat)
    rows = chain(jnp.concatenate([eye, eye_rows(place[1], place[2], own, feat)], axis=0), odd, odd_inv)
    packed[:, feat : 2 * feat] = rows[:own]
    even_inv = matrices(0, even)
    left = dot(halves(rows), order[...]).astype(bf16)
    v = times(left, grads[...])
    both = chain(jnp.concatenate([v, eye], axis=0), even, even_inv)
    packed[:, :feat] = both[2 * own :]

    def columns(group):
        out = both[: 2 * own, :cols]
        for n in range(1, feat // cols):
            out = jnp.where(group == n, both[: 2 * own, n * cols : (n + 1) * cols], out)
        return out

    here, there = columns(place[3]), columns(place[4])
    mine_out[...] = here[:own]
    near_out[...] = here[own:]
    cross_out[...] = there[own:]
    packed[:, 2 * feat :] = there[:own]


def output_kernel(owners, place, packed, got, mine, near, cross, result, store):
    nrow, slots, feat = store.shape
    first = place[5] == 0
    own = mine[:nrow] + near[:nrow]
    other = got[:nrow, 2 * feat :] + cross[:nrow]
    result[:, 0, :] = jnp.where(first, own, other)
    result[:, 1, :] = jnp.where(first, other, own)
    rows = []
    for l in range(2):
        for i in range(2):
            a, b = (packed, got) if l == 0 else (got, packed)
            part = slice(i * feat, (i + 1) * feat)
            rows.append(jnp.where(first, a[:nrow, part], b[:nrow, part]))
    for slot in range(slots):
        acc = jnp.zeros((nrow, feat), f32)
        for f, block in enumerate(rows):
            rank = sum(((owners[e] == owners[f]).astype(jnp.int32) for e in range(f)), jnp.int32(0))
            acc = jnp.where((owners[f] == place[3]) & (rank == slot), block, acc)
        store[:, slot, :] = acc


def shards(activations, back_grads, grads, owners):
    nxl, ncore, nxh, ny, nzh, nzl = (lax.axis_size(a) for a in ("xl", "core", "xh", "y", "zh", "zl"))
    xl, core, xh, y, zh, zl = (lax.axis_index(a) for a in ("xl", "core", "xh", "y", "zh", "zl"))
    nz = nzh * nzl
    layers, tok, feat = activations.shape
    nb = feat // TILE
    nblk = len(upper(nb))
    nrow = grads.shape[1]
    groups = nxl * ncore
    cols = feat // groups
    total = tok * nxl * ncore * nxh * ny * nz
    group = xl * ncore + core
    dp = (xh * ny + y) * nz + zh * nzl + zl
    params = pltpu.CompilerParams(vmem_limit_bytes=48 << 20)
    sm = pl.BlockSpec(memory_space=pltpu.SMEM)
    vm = pl.BlockSpec(memory_space=pltpu.VMEM)
    anywhere = pl.BlockSpec(memory_space=pl.ANY)

    swap = [(0, 1), (1, 0)]
    peer = [lax.ppermute(a, "core", swap) for a in (activations, back_grads)]
    def along(a, axis):
        size = lax.axis_size(axis)
        return [a] + [lax.ppermute(a, axis, [(i, i ^ e) for i in range(size)]) for e in range(1, size)]

    g = lax.dynamic_index_in_dim(grads, core, 0, keepdims=False).astype(bf16)
    g = along(g.reshape(nrow * feat // TILE, TILE), "zh")

    partial = pl.pallas_call(
        factor_kernel,
        out_shape=jax.ShapeDtypeStruct((2 * nblk * TILE, TILE), bf16),
        in_specs=[sm] + [anywhere] * 4,
        out_specs=anywhere,
        scratch_shapes=[
            pltpu.VMEM((2, 2 * tok, feat), bf16),
            pltpu.VMEM((2 * nblk * TILE, TILE), bf16),
            pltpu.SemaphoreType.DMA((2, 3)),
        ],
        compiler_params=pltpu.CompilerParams(vmem_limit_bytes=63 << 20),
        cost_estimate=pl.CostEstimate(flops=4 * tok * 2 * feat * feat, bytes_accessed=8 * tok * feat, transcendentals=0),
    )(core.reshape(1), activations, back_grads, *peer)

    share = nxl * nxh * ny * nzl
    rows = 2 * nblk * TILE // share
    partial, g = lax.optimization_barrier((partial, g))
    terms = lax.all_to_all(partial.reshape(share, rows, TILE), XYL, 0, 0, tiled=True)
    g = along(jnp.stack(g), "y")
    terms, g = lax.optimization_barrier((terms, g))

    mine = jnp.sum(terms.astype(f32), axis=0).astype(bf16)
    mine, g = lax.optimization_barrier((mine, g))
    stack = along(mine, "zh")
    g = jnp.stack(g)
    g = [g, lax.ppermute(g, X, [(0, 3), (3, 0), (1, 2), (2, 1)])]
    stack, g = lax.optimization_barrier((stack, g))
    pair = [a.astype(f32) + b.astype(f32) for a, b in zip(stack[0::2], stack[1::2])]
    factor = (pair[0] + pair[1]) / float(total)
    at = (((xl * nxh + xh) * ny + y) * nzl + zl) * rows + jnp.arange(rows)
    pairs = upper(nb)

    def within(blocks):
        return functools.reduce(jnp.logical_or, [(at // TILE) % nblk == pairs.index((n, n)) for n in blocks])

    spot = jnp.arange(TILE)[None, :]
    on = within(range(nb - 1))[:, None] & ((at % TILE)[:, None] == spot)
    on |= within((0, 1))[:, None] & ((at % TILE - TILE // 2)[:, None] == spot)
    damped = (factor + jnp.where(on, DAMPING, 0.0)).astype(bf16)
    blocks = lax.all_to_all(jnp.broadcast_to(damped[None], (share, rows, TILE)), XYL, 0, 0, tiled=True)
    half = feat // nzl
    part = jnp.stack(g).reshape(half, feat)
    k = jnp.arange(half)
    step = k // nrow
    from_zh = (step % nzh) ^ zh
    from_y = (step // nzh % ny) ^ y
    from_xh = (step // (nzh * ny)) ^ xh
    to = (((from_xh * ny + from_y) * nzh + from_zh) * nzl + zl) * nrow + k % nrow
    order = (jnp.arange(feat)[:, None] == to[None, :]).astype(bf16)

    own = 16
    place = jnp.stack([dp, dp ^ 1, jnp.int32(nrow), group, xl * ncore + 1 - core, core])
    packed, mine, near, cross = pl.pallas_call(
        finish_kernel,
        out_shape=[jax.ShapeDtypeStruct((own, n), f32) for n in (2 * feat + cols, cols, cols, cols)],
        in_specs=[sm, vm, vm, vm],
        out_specs=[vm] * 4,
        scratch_shapes=[pltpu.VMEM((2, 3, feat, feat), bf16)],
        compiler_params=params,
        cost_estimate=pl.CostEstimate(flops=6 * feat**3, bytes_accessed=8 * feat * feat, transcendentals=0),
    )(place, blocks.reshape(2 * nblk * TILE, TILE), part, order)

    got = lax.ppermute(packed, "core", swap)
    near = lax.ppermute(near, "zl", swap)
    cross = lax.ppermute(cross, ("core", "zl"), [(0, 3), (3, 0), (1, 2), (2, 1)])
    result, store = pl.pallas_call(
        output_kernel,
        out_shape=[jax.ShapeDtypeStruct((nrow, layers, cols), f32), jax.ShapeDtypeStruct((nrow, CAP, feat), f32)],
        in_specs=[sm, sm] + [vm] * 5,
        out_specs=[vm, vm],
        compiler_params=params,
    )(owners, place, packed, got, mine, near, cross)
    return jnp.transpose(result, (1, 0, 2)), jnp.transpose(store, (1, 0, 2))


def solution(mesh):
    split = Mesh(mesh.devices.reshape(2, 2, 2, 4, 4, 2), ("xl", "core", "xh", "y", "zh", "zl"))
    grp, dp = ("xl", "core"), ("xh", "y", "zh", "zl")
    return jax.shard_map(
        shards,
        mesh=split,
        in_specs=(P(None, grp + dp, None), P(None, grp + dp, None), P(None, dp, None), P()),
        out_specs=(P(None, dp, grp), P(grp, dp, None)),
        check_vma=False,
    )
```

```python
import functools
import jax
import jax.numpy as jnp
from jax import lax
from jax.experimental import pallas as pl
from jax.experimental.pallas import tpu as pltpu
from jax.sharding import Mesh
from jax.sharding import PartitionSpec as P

CAP = 2
DAMPING = 0.1
TILE = 128
WIDE = 2 * TILE
X = ("xl", "xh")
XYL = ("xl", "xh", "y", "zl")
Z = ("zh", "zl")
bf16 = jnp.bfloat16
f32 = jnp.float32


def upper(nb):
    return [(i, j) for i in range(nb) for j in range(i, nb)][:-1]


def dot(a, b, ca=1, cb=0):
    return lax.dot_general(a, b, (((ca,), (cb,)), ((), ())), preferred_element_type=f32)


def factor_kernel(core_ref, act, bg, peer_act, peer_bg, out, tokens, made, sems):
    tok, feat = act.shape[1:]
    copies = []
    for f, (own, peer) in enumerate(((act, peer_act), (bg, peer_bg))):
        a = pltpu.make_async_copy(own.at[core_ref[0]], tokens.at[f, pl.ds(0, tok)], sems.at[f, 0])
        b = pltpu.make_async_copy(peer.at[core_ref[0]], tokens.at[f, pl.ds(tok, tok)], sems.at[f, 1])
        a.start()
        b.start()
        copies.append((a, b))
    pairs = upper(feat // TILE)
    mid = TILE // 2
    done = []
    for f in range(2):
        for c in copies[f]:
            c.wait()
        for lo in range(0, feat, WIDE):
            r = dot(tokens[f, :, lo : lo + WIDE], tokens[f, :, lo:], 0, 0)
            for top in (0, TILE):
                for left in range(top, feat - lo, TILE):
                    at = (lo + top) // TILE, (lo + left) // TILE
                    block = r[top : top + TILE, left : left + TILE].astype(bf16)
                    if at in pairs:
                        k = f * len(pairs) + pairs.index(at)
                        made[k * TILE : (k + 1) * TILE, :] = block
        for n, quarter in enumerate((block[:mid, :mid], block[mid:, mid:], block[:mid, mid:])):
            k = f * len(pairs) + pairs.index((n, n))
            made[k * TILE + mid : (k + 1) * TILE, :mid] = quarter
        part = pl.ds(f * (made.shape[0] // 2), made.shape[0] // 2)
        done.append(pltpu.make_async_copy(made.at[part], out.at[part], sems.at[f, 2]))
        done[f].start()
    for c in done:
        c.wait()


def halves(u):
    hi = u.astype(bf16)
    return jnp.concatenate([hi, (u - hi.astype(f32)).astype(bf16)], axis=0)


def times(two, m):
    r = dot(two, m)
    n = two.shape[0] // 2
    return r[:n] + r[n:]


def chain(u, mats, inv):
    u = 2.0 * u - times(halves(u), mats[0]) * inv
    u = 2.0 * u - times(halves(u), mats[1])
    u = 2.0 * u - times(halves(u), mats[2])
    t = u - times(halves(u), mats[2])
    t = t - times(halves(t), mats[2])
    return (u + t) * inv


def eye_rows(at, count, own, feat):
    r = lax.broadcasted_iota(jnp.int32, (own, feat), 0)
    c = lax.broadcasted_iota(jnp.int32, (own, feat), 1)
    return jnp.where((c == at * count + r) & (r < count), 1.0, 0.0).astype(f32)


def finish_kernel(place, blocks, grads, order, packed, mine_out, near_out, cross_out, mats):
    feat = order.shape[0]
    pairs = upper(feat // TILE)
    mid = TILE // 2

    def put(dst, i, j, block):
        n = block.shape[0]
        dst[i * n : (i + 1) * n, j * n : (j + 1) * n] = block
        if i != j:
            dst[j * n : (j + 1) * n, i * n : (i + 1) * n] = block.T

    def square(src, dst, one, two):
        for i in range(feat // WIDE):
            lo = i * WIDE
            r = dot(src[lo : lo + WIDE, :], src[:, lo:])
            for j in range(i, feat // WIDE):
                old = src[lo : lo + WIDE, j * WIDE : (j + 1) * WIDE].astype(f32)
                new = one * old - two * r[:, (j - i) * WIDE : (j - i + 1) * WIDE]
                put(dst, i, j, new.astype(bf16))

    def matrices(f, mats):
        corner = []
        for n, (i, j) in enumerate(pairs):
            k = f * len(pairs) + n
            block = blocks[k * TILE : (k + 1) * TILE, :]
            if i == j and i < 3:
                up = block[:mid, mid:]
                corner.append(block[mid:, :mid])
                low = jnp.concatenate([up.T, block[mid:, mid:]], axis=1)
                block = jnp.concatenate([block[:mid], low], axis=0)
            put(mats.at[0], i, j, block)
        first, last, up = corner
        low = jnp.concatenate([up.T, last], axis=1)
        block = jnp.concatenate([jnp.concatenate([first, up], axis=1), low], axis=0)
        put(mats.at[0], feat // TILE - 1, feat // TILE - 1, block)
        sums = jnp.sum(jnp.abs(mats[0].astype(f32)), axis=1, keepdims=True)
        inv = 1.0 / jnp.max(sums, axis=0, keepdims=True)
        square(mats.at[0], mats.at[1], 2.0 * inv, inv * inv)
        square(mats.at[1], mats.at[2], 2.0, 1.0)
        return inv

    even, odd = mats.at[0], mats.at[1]
    odd_inv = matrices(1, odd)
    own = packed.shape[0]
    cols = mine_out.shape[1]
    eye = eye_rows(place[0], place[2], own, feat)
    rows = chain(jnp.concatenate([eye, eye_rows(place[1], place[2], own, feat)], axis=0), odd, odd_inv)
    packed[:, feat : 2 * feat] = rows[:own]
    even_inv = matrices(0, even)
    left = dot(halves(rows), order[...]).astype(bf16)
    v = times(left, grads[...])
    both = chain(jnp.concatenate([v, eye], axis=0), even, even_inv)
    packed[:, :feat] = both[2 * own :]

    def columns(group):
        out = both[: 2 * own, :cols]
        for n in range(1, feat // cols):
            out = jnp.where(group == n, both[: 2 * own, n * cols : (n + 1) * cols], out)
        return out

    here, there = columns(place[3]), columns(place[4])
    mine_out[...] = here[:own]
    near_out[...] = here[own:]
    cross_out[...] = there[own:]
    packed[:, 2 * feat :] = there[:own]


def output_kernel(owners, place, packed, got, mine, near, cross, result, store):
    nrow, slots, feat = store.shape
    first = place[5] == 0
    own = mine[:nrow] + near[:nrow]
    other = got[:nrow, 2 * feat :] + cross[:nrow]
    result[:, 0, :] = jnp.where(first, own, other)
    result[:, 1, :] = jnp.where(first, other, own)
    rows = []
    for l in range(2):
        for i in range(2):
            a, b = (packed, got) if l == 0 else (got, packed)
            part = slice(i * feat, (i + 1) * feat)
            rows.append(jnp.where(first, a[:nrow, part], b[:nrow, part]))
    for slot in range(slots):
        acc = jnp.zeros((nrow, feat), f32)
        for f, block in enumerate(rows):
            rank = sum(((owners[e] == owners[f]).astype(jnp.int32) for e in range(f)), jnp.int32(0))
            acc = jnp.where((owners[f] == place[3]) & (rank == slot), block, acc)
        store[:, slot, :] = acc


def shards(activations, back_grads, grads, owners):
    nxl, ncore, nxh, ny, nzh, nzl = (lax.axis_size(a) for a in ("xl", "core", "xh", "y", "zh", "zl"))
    xl, core, xh, y, zh, zl = (lax.axis_index(a) for a in ("xl", "core", "xh", "y", "zh", "zl"))
    nz = nzh * nzl
    layers, tok, feat = activations.shape
    nb = feat // TILE
    nblk = len(upper(nb))
    nrow = grads.shape[1]
    groups = nxl * ncore
    cols = feat // groups
    total = tok * nxl * ncore * nxh * ny * nz
    group = xl * ncore + core
    dp = (xh * ny + y) * nz + zh * nzl + zl
    params = pltpu.CompilerParams(vmem_limit_bytes=48 << 20)
    sm = pl.BlockSpec(memory_space=pltpu.SMEM)
    vm = pl.BlockSpec(memory_space=pltpu.VMEM)
    anywhere = pl.BlockSpec(memory_space=pl.ANY)

    swap = [(0, 1), (1, 0)]
    peer = [lax.ppermute(a, "core", swap) for a in (activations, back_grads)]
    def along(a, axis):
        size = lax.axis_size(axis)
        return [a] + [lax.ppermute(a, axis, [(i, i ^ e) for i in range(size)]) for e in range(1, size)]

    g = lax.dynamic_index_in_dim(grads, core, 0, keepdims=False).astype(bf16)
    g = along(g.reshape(nrow * feat // TILE, TILE), "zh")

    partial = pl.pallas_call(
        factor_kernel,
        out_shape=jax.ShapeDtypeStruct((2 * nblk * TILE, TILE), bf16),
        in_specs=[sm] + [anywhere] * 4,
        out_specs=anywhere,
        scratch_shapes=[
            pltpu.VMEM((2, 2 * tok, feat), bf16),
            pltpu.VMEM((2 * nblk * TILE, TILE), bf16),
            pltpu.SemaphoreType.DMA((2, 3)),
        ],
        compiler_params=pltpu.CompilerParams(vmem_limit_bytes=63 << 20),
        cost_estimate=pl.CostEstimate(flops=4 * tok * 2 * feat * feat, bytes_accessed=8 * tok * feat, transcendentals=0),
    )(core.reshape(1), activations, back_grads, *peer)

    share = nxl * nxh * ny * nzl
    rows = 2 * nblk * TILE // share
    partial, g = lax.optimization_barrier((partial, g))
    terms = lax.all_to_all(partial.reshape(share, rows, TILE), XYL, 0, 0, tiled=True)
    g = along(jnp.stack(g), "y")

    mine = jnp.sum(terms.astype(f32), axis=0).astype(bf16)
    stack = along(mine, "zh")
    g = jnp.stack(g)
    g = [g, lax.ppermute(g, X, [(0, 3), (3, 0), (1, 2), (2, 1)])]
    stack, g = lax.optimization_barrier((stack, g))
    pair = [a.astype(f32) + b.astype(f32) for a, b in zip(stack[0::2], stack[1::2])]
    factor = (pair[0] + pair[1]) / float(total)
    at = (((xl * nxh + xh) * ny + y) * nzl + zl) * rows + jnp.arange(rows)
    pairs = upper(nb)

    def within(blocks):
        return functools.reduce(jnp.logical_or, [(at // TILE) % nblk == pairs.index((n, n)) for n in blocks])

    spot = jnp.arange(TILE)[None, :]
    on = within(range(nb - 1))[:, None] & ((at % TILE)[:, None] == spot)
    on |= within((0, 1))[:, None] & ((at % TILE - TILE // 2)[:, None] == spot)
    damped = (factor + jnp.where(on, DAMPING, 0.0)).astype(bf16)
    blocks = lax.all_to_all(jnp.broadcast_to(damped[None], (share, rows, TILE)), XYL, 0, 0, tiled=True)
    half = feat // nzl
    part = jnp.stack(g).reshape(half, feat)
    k = jnp.arange(half)
    step = k // nrow
    from_zh = (step % nzh) ^ zh
    from_y = (step // nzh % ny) ^ y
    from_xh = (step // (nzh * ny)) ^ xh
    to = (((from_xh * ny + from_y) * nzh + from_zh) * nzl + zl) * nrow + k % nrow
    order = (jnp.arange(feat)[:, None] == to[None, :]).astype(bf16)

    own = 16
    place = jnp.stack([dp, dp ^ 1, jnp.int32(nrow), group, xl * ncore + 1 - core, core])
    packed, mine, near, cross = pl.pallas_call(
        finish_kernel,
        out_shape=[jax.ShapeDtypeStruct((own, n), f32) for n in (2 * feat + cols, cols, cols, cols)],
        in_specs=[sm, vm, vm, vm],
        out_specs=[vm] * 4,
        scratch_shapes=[pltpu.VMEM((2, 3, feat, feat), bf16)],
        compiler_params=params,
        cost_estimate=pl.CostEstimate(flops=6 * feat**3, bytes_accessed=8 * feat * feat, transcendentals=0),
    )(place, blocks.reshape(2 * nblk * TILE, TILE), part, order)

    got = lax.ppermute(packed, "core", swap)
    near = lax.ppermute(near, "zl", swap)
    cross = lax.ppermute(cross, ("core", "zl"), [(0, 3), (3, 0), (1, 2), (2, 1)])
    result, store = pl.pallas_call(
        output_kernel,
        out_shape=[jax.ShapeDtypeStruct((nrow, layers, cols), f32), jax.ShapeDtypeStruct((nrow, CAP, feat), f32)],
        in_specs=[sm, sm] + [vm] * 5,
        out_specs=[vm, vm],
        compiler_params=params,
    )(owners, place, packed, got, mine, near, cross)
    return jnp.transpose(result, (1, 0, 2)), jnp.transpose(store, (1, 0, 2))


def solution(mesh):
    split = Mesh(mesh.devices.reshape(2, 2, 2, 4, 4, 2), ("xl", "core", "xh", "y", "zh", "zl"))
    grp, dp = ("xl", "core"), ("xh", "y", "zh", "zl")
    return jax.shard_map(
        shards,
        mesh=split,
        in_specs=(P(None, grp + dp, None), P(None, grp + dp, None), P(None, dp, None), P()),
        out_specs=(P(None, dp, grp), P(grp, dp, None)),
        check_vma=False,
    )
```

```python
import functools
import jax
import jax.numpy as jnp
from jax import lax
from jax.experimental import pallas as pl
from jax.experimental.pallas import tpu as pltpu
from jax.sharding import Mesh
from jax.sharding import PartitionSpec as P

CAP = 2
DAMPING = 0.1
TILE = 128
WIDE = 2 * TILE
X = ("xl", "xh")
XYL = ("xl", "xh", "y", "zl")
Z = ("zh", "zl")
bf16 = jnp.bfloat16
f32 = jnp.float32


def upper(nb):
    return [(i, j) for i in range(nb) for j in range(i, nb)][:-1]


def dot(a, b, ca=1, cb=0):
    return lax.dot_general(a, b, (((ca,), (cb,)), ((), ())), preferred_element_type=f32)


def factor_kernel(core_ref, act, bg, peer_act, peer_bg, out, tokens, made, sems):
    tok, feat = act.shape[1:]
    copies = []
    for f, (own, peer) in enumerate(((act, peer_act), (bg, peer_bg))):
        a = pltpu.make_async_copy(own.at[core_ref[0]], tokens.at[f, pl.ds(0, tok)], sems.at[f, 0])
        b = pltpu.make_async_copy(peer.at[core_ref[0]], tokens.at[f, pl.ds(tok, tok)], sems.at[f, 1])
        a.start()
        b.start()
        copies.append((a, b))
    pairs = upper(feat // TILE)
    mid = TILE // 2
    done = []
    for f in range(2):
        for c in copies[f]:
            c.wait()
        for lo in range(0, feat, WIDE):
            r = dot(tokens[f, :, lo : lo + WIDE], tokens[f, :, lo:], 0, 0)
            for top in (0, TILE):
                for left in range(top, feat - lo, TILE):
                    at = (lo + top) // TILE, (lo + left) // TILE
                    block = r[top : top + TILE, left : left + TILE].astype(bf16)
                    if at in pairs:
                        k = f * len(pairs) + pairs.index(at)
                        made[k * TILE : (k + 1) * TILE, :] = block
        for n, quarter in enumerate((block[:mid, :mid], block[mid:, mid:], block[:mid, mid:])):
            k = f * len(pairs) + pairs.index((n, n))
            made[k * TILE + mid : (k + 1) * TILE, :mid] = quarter
        part = pl.ds(f * (made.shape[0] // 2), made.shape[0] // 2)
        done.append(pltpu.make_async_copy(made.at[part], out.at[part], sems.at[f, 2]))
        done[f].start()
    for c in done:
        c.wait()


def halves(u):
    hi = u.astype(bf16)
    return jnp.concatenate([hi, (u - hi.astype(f32)).astype(bf16)], axis=0)


def times(two, m):
    r = dot(two, m)
    n = two.shape[0] // 2
    return r[:n] + r[n:]


def chain(u, mats, inv):
    u = 2.0 * u - times(halves(u), mats[0]) * inv
    u = 2.0 * u - times(halves(u), mats[1])
    u = 2.0 * u - times(halves(u), mats[2])
    t = u - times(halves(u), mats[2])
    t = t - times(halves(t), mats[2])
    return (u + t) * inv


def eye_rows(at, count, own, feat):
    r = lax.broadcasted_iota(jnp.int32, (own, feat), 0)
    c = lax.broadcasted_iota(jnp.int32, (own, feat), 1)
    return jnp.where((c == at * count + r) & (r < count), 1.0, 0.0).astype(f32)


def finish_kernel(place, blocks, grads, packed, mine_out, near_out, cross_out, mats):
    feat = grads.shape[0]
    pairs = upper(feat // TILE)
    mid = TILE // 2

    def put(dst, i, j, block):
        n = block.shape[0]
        dst[i * n : (i + 1) * n, j * n : (j + 1) * n] = block
        if i != j:
            dst[j * n : (j + 1) * n, i * n : (i + 1) * n] = block.T

    def square(src, dst, one, two):
        for i in range(feat // WIDE):
            lo = i * WIDE
            r = dot(src[lo : lo + WIDE, :], src[:, lo:])
            for j in range(i, feat // WIDE):
                old = src[lo : lo + WIDE, j * WIDE : (j + 1) * WIDE].astype(f32)
                new = one * old - two * r[:, (j - i) * WIDE : (j - i + 1) * WIDE]
                put(dst, i, j, new.astype(bf16))

    def matrices(f, mats):
        corner = []
        for n, (i, j) in enumerate(pairs):
            k = f * len(pairs) + n
            block = blocks[k * TILE : (k + 1) * TILE, :]
            if i == j and i < 3:
                up = block[:mid, mid:]
                corner.append(block[mid:, :mid])
                low = jnp.concatenate([up.T, block[mid:, mid:]], axis=1)
                block = jnp.concatenate([block[:mid], low], axis=0)
            put(mats.at[0], i, j, block)
        first, last, up = corner
        low = jnp.concatenate([up.T, last], axis=1)
        block = jnp.concatenate([jnp.concatenate([first, up], axis=1), low], axis=0)
        put(mats.at[0], feat // TILE - 1, feat // TILE - 1, block)
        sums = jnp.sum(jnp.abs(mats[0].astype(f32)), axis=1, keepdims=True)
        inv = 1.0 / jnp.max(sums, axis=0, keepdims=True)
        square(mats.at[0], mats.at[1], 2.0 * inv, inv * inv)
        square(mats.at[1], mats.at[2], 2.0, 1.0)
        return inv

    even, odd = mats.at[0], mats.at[1]
    odd_inv = matrices(1, odd)
    own = packed.shape[0]
    cols = mine_out.shape[1]
    eye = eye_rows(place[0], place[2], own, feat)
    rows = chain(jnp.concatenate([eye, eye_rows(place[1], place[2], own, feat)], axis=0), odd, odd_inv)
    packed[:, feat : 2 * feat] = rows[:own]
    even_inv = matrices(0, even)
    v = times(halves(rows), grads[...])
    both = chain(jnp.concatenate([v, eye], axis=0), even, even_inv)
    packed[:, :feat] = both[2 * own :]

    def columns(group):
        out = both[: 2 * own, :cols]
        for n in range(1, feat // cols):
            out = jnp.where(group == n, both[: 2 * own, n * cols : (n + 1) * cols], out)
        return out

    here, there = columns(place[3]), columns(place[4])
    mine_out[...] = here[:own]
    near_out[...] = here[own:]
    cross_out[...] = there[own:]
    packed[:, 2 * feat :] = there[:own]


def output_kernel(owners, place, packed, got, mine, near, cross, result, store):
    nrow, slots, feat = store.shape
    first = place[5] == 0
    own = mine[:nrow] + near[:nrow]
    other = got[:nrow, 2 * feat :] + cross[:nrow]
    result[:, 0, :] = jnp.where(first, own, other)
    result[:, 1, :] = jnp.where(first, other, own)
    rows = []
    for l in range(2):
        for i in range(2):
            a, b = (packed, got) if l == 0 else (got, packed)
            part = slice(i * feat, (i + 1) * feat)
            rows.append(jnp.where(first, a[:nrow, part], b[:nrow, part]))
    for slot in range(slots):
        acc = jnp.zeros((nrow, feat), f32)
        for f, block in enumerate(rows):
            rank = sum(((owners[e] == owners[f]).astype(jnp.int32) for e in range(f)), jnp.int32(0))
            acc = jnp.where((owners[f] == place[3]) & (rank == slot), block, acc)
        store[:, slot, :] = acc


def shards(activations, back_grads, grads, owners):
    nxl, ncore, nxh, ny, nzh, nzl = (lax.axis_size(a) for a in ("xl", "core", "xh", "y", "zh", "zl"))
    xl, core, xh, y, zh, zl = (lax.axis_index(a) for a in ("xl", "core", "xh", "y", "zh", "zl"))
    nz = nzh * nzl
    layers, tok, feat = activations.shape
    nb = feat // TILE
    nblk = len(upper(nb))
    nrow = grads.shape[1]
    groups = nxl * ncore
    cols = feat // groups
    total = tok * nxl * ncore * nxh * ny * nz
    group = xl * ncore + core
    dp = (xh * ny + y) * nz + zh * nzl + zl
    params = pltpu.CompilerParams(vmem_limit_bytes=48 << 20)
    sm = pl.BlockSpec(memory_space=pltpu.SMEM)
    vm = pl.BlockSpec(memory_space=pltpu.VMEM)
    anywhere = pl.BlockSpec(memory_space=pl.ANY)

    swap = [(0, 1), (1, 0)]
    peer = [lax.ppermute(a, "core", swap) for a in (activations, back_grads)]
    def along(a, axis):
        size = lax.axis_size(axis)
        return [a] + [lax.ppermute(a, axis, [(i, i ^ e) for i in range(size)]) for e in range(1, size)]

    g = lax.dynamic_index_in_dim(grads, core, 0, keepdims=False).astype(bf16)
    g = along(g.reshape(nrow * feat // TILE, TILE), "zh")

    partial = pl.pallas_call(
        factor_kernel,
        out_shape=jax.ShapeDtypeStruct((2 * nblk * TILE, TILE), bf16),
        in_specs=[sm] + [anywhere] * 4,
        out_specs=anywhere,
        scratch_shapes=[
            pltpu.VMEM((2, 2 * tok, feat), bf16),
            pltpu.VMEM((2 * nblk * TILE, TILE), bf16),
            pltpu.SemaphoreType.DMA((2, 3)),
        ],
        compiler_params=pltpu.CompilerParams(vmem_limit_bytes=63 << 20),
        cost_estimate=pl.CostEstimate(flops=4 * tok * 2 * feat * feat, bytes_accessed=8 * tok * feat, transcendentals=0),
    )(core.reshape(1), activations, back_grads, *peer)

    share = nxl * nxh * ny * nzl
    rows = 2 * nblk * TILE // share
    partial, g = lax.optimization_barrier((partial, g))
    terms = lax.all_to_all(partial.reshape(share, rows, TILE), XYL, 0, 0, tiled=True)
    g = along(jnp.stack(g), "y")

    mine = jnp.sum(terms.astype(f32), axis=0).astype(bf16)
    stack = along(mine, "zh")
    g = jnp.stack(g)
    g = [g, lax.ppermute(g, X, [(0, 3), (3, 0), (1, 2), (2, 1)])]
    stack, g = lax.optimization_barrier((stack, g))
    pair = [a.astype(f32) + b.astype(f32) for a, b in zip(stack[0::2], stack[1::2])]
    factor = (pair[0] + pair[1]) / float(total)
    at = (((xl * nxh + xh) * ny + y) * nzl + zl) * rows + jnp.arange(rows)
    pairs = upper(nb)

    def within(blocks):
        return functools.reduce(jnp.logical_or, [(at // TILE) % nblk == pairs.index((n, n)) for n in blocks])

    spot = jnp.arange(TILE)[None, :]
    on = within(range(nb - 1))[:, None] & ((at % TILE)[:, None] == spot)
    on |= within((0, 1))[:, None] & ((at % TILE - TILE // 2)[:, None] == spot)
    damped = (factor + jnp.where(on, DAMPING, 0.0)).astype(bf16)
    blocks = lax.all_to_all(jnp.broadcast_to(damped[None], (share, rows, TILE)), XYL, 0, 0, tiled=True)
    half = feat // nzl
    part = jnp.stack(g).reshape(half, feat)
    k = jnp.arange(half)
    step = k // nrow
    from_zh = (step % nzh) ^ zh
    from_y = (step // nzh % ny) ^ y
    from_xh = (step // (nzh * ny)) ^ xh
    to = (((from_xh * ny + from_y) * nzh + from_zh) * nzl + zl) * nrow + k % nrow
    order = (jnp.arange(feat)[:, None] == to[None, :]).astype(bf16)
    whole = dot(order, part).astype(bf16)

    own = 16
    place = jnp.stack([dp, dp ^ 1, jnp.int32(nrow), group, xl * ncore + 1 - core, core])
    packed, mine, near, cross = pl.pallas_call(
        finish_kernel,
        out_shape=[jax.ShapeDtypeStruct((own, n), f32) for n in (2 * feat + cols, cols, cols, cols)],
        in_specs=[sm, vm, vm],
        out_specs=[vm] * 4,
        scratch_shapes=[pltpu.VMEM((2, 3, feat, feat), bf16)],
        compiler_params=params,
        cost_estimate=pl.CostEstimate(flops=6 * feat**3, bytes_accessed=8 * feat * feat, transcendentals=0),
    )(place, blocks.reshape(2 * nblk * TILE, TILE), whole)

    got = lax.ppermute(packed, "core", swap)
    near = lax.ppermute(near, "zl", swap)
    cross = lax.ppermute(cross, ("core", "zl"), [(0, 3), (3, 0), (1, 2), (2, 1)])
    result, store = pl.pallas_call(
        output_kernel,
        out_shape=[jax.ShapeDtypeStruct((nrow, layers, cols), f32), jax.ShapeDtypeStruct((nrow, CAP, feat), f32)],
        in_specs=[sm, sm] + [vm] * 5,
        out_specs=[vm, vm],
        compiler_params=params,
    )(owners, place, packed, got, mine, near, cross)
    return jnp.transpose(result, (1, 0, 2)), jnp.transpose(store, (1, 0, 2))


def solution(mesh):
    split = Mesh(mesh.devices.reshape(2, 2, 2, 4, 4, 2), ("xl", "core", "xh", "y", "zh", "zl"))
    grp, dp = ("xl", "core"), ("xh", "y", "zh", "zl")
    return jax.shard_map(
        shards,
        mesh=split,
        in_specs=(P(None, grp + dp, None), P(None, grp + dp, None), P(None, dp, None), P()),
        out_specs=(P(None, dp, grp), P(grp, dp, None)),
        check_vma=False,
    )
```

```python
import functools
import jax
import jax.numpy as jnp
from jax import lax
from jax.experimental import pallas as pl
from jax.experimental.pallas import tpu as pltpu
from jax.sharding import Mesh
from jax.sharding import PartitionSpec as P

CAP = 2
DAMPING = 0.1
TILE = 128
WIDE = 2 * TILE
X = ("xl", "xh")
XYL = ("xl", "xh", "y", "zl")
Z = ("zh", "zl")
bf16 = jnp.bfloat16
f32 = jnp.float32


def upper(nb):
    return [(i, j) for i in range(nb) for j in range(i, nb)][:-1]


def dot(a, b, ca=1, cb=0):
    return lax.dot_general(a, b, (((ca,), (cb,)), ((), ())), preferred_element_type=f32)


def factor_kernel(core_ref, act, bg, peer_act, peer_bg, out, tokens, made, sems):
    tok, feat = act.shape[1:]
    copies = []
    for f, (own, peer) in enumerate(((act, peer_act), (bg, peer_bg))):
        a = pltpu.make_async_copy(own.at[core_ref[0]], tokens.at[f, pl.ds(0, tok)], sems.at[f, 0])
        b = pltpu.make_async_copy(peer.at[core_ref[0]], tokens.at[f, pl.ds(tok, tok)], sems.at[f, 1])
        a.start()
        b.start()
        copies.append((a, b))
    pairs = upper(feat // TILE)
    mid = TILE // 2
    done = []
    for f in range(2):
        for c in copies[f]:
            c.wait()
        for lo in range(0, feat, WIDE):
            r = dot(tokens[f, :, lo : lo + WIDE], tokens[f, :, lo:], 0, 0)
            for top in (0, TILE):
                for left in range(top, feat - lo, TILE):
                    at = (lo + top) // TILE, (lo + left) // TILE
                    block = r[top : top + TILE, left : left + TILE].astype(bf16)
                    if at in pairs:
                        k = f * len(pairs) + pairs.index(at)
                        made[k * TILE : (k + 1) * TILE, :] = block
        for n, quarter in enumerate((block[:mid, :mid], block[mid:, mid:], block[:mid, mid:])):
            k = f * len(pairs) + pairs.index((n, n))
            made[k * TILE + mid : (k + 1) * TILE, :mid] = quarter
        part = pl.ds(f * (made.shape[0] // 2), made.shape[0] // 2)
        done.append(pltpu.make_async_copy(made.at[part], out.at[part], sems.at[f, 2]))
        done[f].start()
    for c in done:
        c.wait()


def halves(u):
    hi = u.astype(bf16)
    return jnp.concatenate([hi, (u - hi.astype(f32)).astype(bf16)], axis=0)


def times(two, m):
    r = dot(two, m)
    n = two.shape[0] // 2
    return r[:n] + r[n:]


def chain(u, mats, inv):
    u = 2.0 * u - times(halves(u), mats[0]) * inv
    u = 2.0 * u - times(halves(u), mats[1])
    u = 2.0 * u - times(halves(u), mats[2])
    t = u - times(halves(u), mats[2])
    t = t - times(halves(t), mats[2])
    return (u + t) * inv


def eye_rows(at, count, own, feat):
    r = lax.broadcasted_iota(jnp.int32, (own, feat), 0)
    c = lax.broadcasted_iota(jnp.int32, (own, feat), 1)
    return jnp.where((c == at * count + r) & (r < count), 1.0, 0.0).astype(f32)


def finish_kernel(place, blocks, grads, packed, mine_out, near_out, cross_out, mats):
    feat = grads.shape[0]
    pairs = upper(feat // TILE)
    mid = TILE // 2

    def put(dst, i, j, block):
        n = block.shape[0]
        dst[i * n : (i + 1) * n, j * n : (j + 1) * n] = block
        if i != j:
            dst[j * n : (j + 1) * n, i * n : (i + 1) * n] = block.T

    def square(src, dst, one, two):
        for i in range(feat // WIDE):
            lo = i * WIDE
            r = dot(src[lo : lo + WIDE, :], src[:, lo:])
            for j in range(i, feat // WIDE):
                old = src[lo : lo + WIDE, j * WIDE : (j + 1) * WIDE].astype(f32)
                new = one * old - two * r[:, (j - i) * WIDE : (j - i + 1) * WIDE]
                put(dst, i, j, new.astype(bf16))

    def matrices(f, mats):
        corner = []
        for n, (i, j) in enumerate(pairs):
            k = f * len(pairs) + n
            block = blocks[k * TILE : (k + 1) * TILE, :]
            if i == j and i < 3:
                up = block[:mid, mid:]
                corner.append(block[mid:, :mid])
                low = jnp.concatenate([up.T, block[mid:, mid:]], axis=1)
                block = jnp.concatenate([block[:mid], low], axis=0)
            put(mats.at[0], i, j, block)
        first, last, up = corner
        low = jnp.concatenate([up.T, last], axis=1)
        block = jnp.concatenate([jnp.concatenate([first, up], axis=1), low], axis=0)
        put(mats.at[0], feat // TILE - 1, feat // TILE - 1, block)
        sums = jnp.sum(jnp.abs(mats[0].astype(f32)), axis=1, keepdims=True)
        inv = 1.0 / jnp.max(sums, axis=0, keepdims=True)
        square(mats.at[0], mats.at[1], 2.0 * inv, inv * inv)
        square(mats.at[1], mats.at[2], 2.0, 1.0)
        return inv

    even, odd = mats.at[0], mats.at[1]
    odd_inv = matrices(1, odd)
    own = packed.shape[0]
    cols = mine_out.shape[1]
    eye = eye_rows(place[0], place[2], own, feat)
    rows = chain(jnp.concatenate([eye, eye_rows(place[1], place[2], own, feat)], axis=0), odd, odd_inv)
    packed[:, feat : 2 * feat] = rows[:own]
    even_inv = matrices(0, even)
    v = times(halves(rows), grads[...])
    both = chain(jnp.concatenate([v, eye], axis=0), even, even_inv)
    packed[:, :feat] = both[2 * own :]

    def columns(group):
        out = both[: 2 * own, :cols]
        for n in range(1, feat // cols):
            out = jnp.where(group == n, both[: 2 * own, n * cols : (n + 1) * cols], out)
        return out

    here, there = columns(place[3]), columns(place[4])
    mine_out[...] = here[:own]
    near_out[...] = here[own:]
    cross_out[...] = there[own:]
    packed[:, 2 * feat :] = there[:own]


def output_kernel(owners, place, packed, got, mine, near, cross, result, store):
    nrow, slots, feat = store.shape
    first = place[5] == 0
    own = mine[:nrow] + near[:nrow]
    other = got[:nrow, 2 * feat :] + cross[:nrow]
    result[:, 0, :] = jnp.where(first, own, other)
    result[:, 1, :] = jnp.where(first, other, own)
    rows = []
    for l in range(2):
        for i in range(2):
            a, b = (packed, got) if l == 0 else (got, packed)
            part = slice(i * feat, (i + 1) * feat)
            rows.append(jnp.where(first, a[:nrow, part], b[:nrow, part]))
    for slot in range(slots):
        acc = jnp.zeros((nrow, feat), f32)
        for f, block in enumerate(rows):
            rank = sum(((owners[e] == owners[f]).astype(jnp.int32) for e in range(f)), jnp.int32(0))
            acc = jnp.where((owners[f] == place[3]) & (rank == slot), block, acc)
        store[:, slot, :] = acc


def shards(activations, back_grads, grads, owners):
    nxl, ncore, nxh, ny, nzh, nzl = (lax.axis_size(a) for a in ("xl", "core", "xh", "y", "zh", "zl"))
    xl, core, xh, y, zh, zl = (lax.axis_index(a) for a in ("xl", "core", "xh", "y", "zh", "zl"))
    nz = nzh * nzl
    layers, tok, feat = activations.shape
    nb = feat // TILE
    nblk = len(upper(nb))
    nrow = grads.shape[1]
    groups = nxl * ncore
    cols = feat // groups
    total = tok * nxl * ncore * nxh * ny * nz
    group = xl * ncore + core
    dp = (xh * ny + y) * nz + zh * nzl + zl
    params = pltpu.CompilerParams(vmem_limit_bytes=48 << 20)
    sm = pl.BlockSpec(memory_space=pltpu.SMEM)
    vm = pl.BlockSpec(memory_space=pltpu.VMEM)
    anywhere = pl.BlockSpec(memory_space=pl.ANY)

    swap = [(0, 1), (1, 0)]
    peer = [lax.ppermute(a, "core", swap) for a in (activations, back_grads)]
    def along(a, axis):
        size = lax.axis_size(axis)
        return [a] + [lax.ppermute(a, axis, [(i, i ^ e) for i in range(size)]) for e in range(1, size)]

    g = lax.dynamic_index_in_dim(grads, core, 0, keepdims=False).astype(bf16)
    g = along(g.reshape(nrow * feat // TILE, TILE), "zh")

    partial = pl.pallas_call(
        factor_kernel,
        out_shape=jax.ShapeDtypeStruct((2 * nblk * TILE, TILE), bf16),
        in_specs=[sm] + [anywhere] * 4,
        out_specs=anywhere,
        scratch_shapes=[
            pltpu.VMEM((2, 2 * tok, feat), bf16),
            pltpu.VMEM((2 * nblk * TILE, TILE), bf16),
            pltpu.SemaphoreType.DMA((2, 3)),
        ],
        compiler_params=pltpu.CompilerParams(vmem_limit_bytes=63 << 20),
        cost_estimate=pl.CostEstimate(flops=4 * tok * 2 * feat * feat, bytes_accessed=8 * tok * feat, transcendentals=0),
    )(core.reshape(1), activations, back_grads, *peer)

    share = nxl * nxh * ny * nzl
    rows = 2 * nblk * TILE // share
    partial, g = lax.optimization_barrier((partial, g))
    terms = lax.all_to_all(partial.reshape(share, rows, TILE), XYL, 0, 0, tiled=True)
    g = along(jnp.stack(g), "y")

    mine = jnp.sum(terms.astype(f32), axis=0).astype(bf16)
    stack = along(mine, "zh")
    g = jnp.stack(g)
    g = [g, lax.ppermute(g, X, [(0, 3), (3, 0), (1, 2), (2, 1)])]
    stack, g = lax.optimization_barrier((stack, g))
    pair = [a.astype(f32) + b.astype(f32) for a, b in zip(stack[0::2], stack[1::2])]
    factor = (pair[0] + pair[1]) / float(total)
    at = (((xl * nxh + xh) * ny + y) * nzl + zl) * rows + jnp.arange(rows)
    pairs = upper(nb)

    def within(blocks):
        return functools.reduce(jnp.logical_or, [(at // TILE) % nblk == pairs.index((n, n)) for n in blocks])

    spot = jnp.arange(TILE)[None, :]
    on = within(range(nb - 1))[:, None] & ((at % TILE)[:, None] == spot)
    on |= within((0, 1))[:, None] & ((at % TILE - TILE // 2)[:, None] == spot)
    damped = jnp.broadcast_to((factor + jnp.where(on, DAMPING, 0.0))[None], (share, rows, TILE)).astype(bf16)
    blocks = lax.all_to_all(damped, XYL, 0, 0, tiled=True)
    half = feat // nzl
    part = jnp.stack(g).reshape(half, feat)
    k = jnp.arange(half)
    step = k // nrow
    from_zh = (step % nzh) ^ zh
    from_y = (step // nzh % ny) ^ y
    from_xh = (step // (nzh * ny)) ^ xh
    to = (((from_xh * ny + from_y) * nzh + from_zh) * nzl + zl) * nrow + k % nrow
    order = (jnp.arange(feat)[:, None] == to[None, :]).astype(bf16)
    whole = dot(order, part).astype(bf16)

    own = 16
    place = jnp.stack([dp, dp ^ 1, jnp.int32(nrow), group, xl * ncore + 1 - core, core])
    packed, mine, near, cross = pl.pallas_call(
        finish_kernel,
        out_shape=[jax.ShapeDtypeStruct((own, n), f32) for n in (2 * feat + cols, cols, cols, cols)],
        in_specs=[sm, vm, vm],
        out_specs=[vm] * 4,
        scratch_shapes=[pltpu.VMEM((2, 3, feat, feat), bf16)],
        compiler_params=params,
        cost_estimate=pl.CostEstimate(flops=6 * feat**3, bytes_accessed=8 * feat * feat, transcendentals=0),
    )(place, blocks.reshape(2 * nblk * TILE, TILE), whole)

    got = lax.ppermute(packed, "core", swap)
    near = lax.ppermute(near, "zl", swap)
    cross = lax.ppermute(cross, ("core", "zl"), [(0, 3), (3, 0), (1, 2), (2, 1)])
    result, store = pl.pallas_call(
        output_kernel,
        out_shape=[jax.ShapeDtypeStruct((nrow, layers, cols), f32), jax.ShapeDtypeStruct((nrow, CAP, feat), f32)],
        in_specs=[sm, sm] + [vm] * 5,
        out_specs=[vm, vm],
        compiler_params=params,
    )(owners, place, packed, got, mine, near, cross)
    return jnp.transpose(result, (1, 0, 2)), jnp.transpose(store, (1, 0, 2))


def solution(mesh):
    split = Mesh(mesh.devices.reshape(2, 2, 2, 4, 4, 2), ("xl", "core", "xh", "y", "zh", "zl"))
    grp, dp = ("xl", "core"), ("xh", "y", "zh", "zl")
    return jax.shard_map(
        shards,
        mesh=split,
        in_specs=(P(None, grp + dp, None), P(None, grp + dp, None), P(None, dp, None), P()),
        out_specs=(P(None, dp, grp), P(grp, dp, None)),
        check_vma=False,
    )
```
